256 devices in a mesh: row: 8 (over x, core), col: 32 (over y, z).
Axes of the slice: x: 4, y: 4, z: 8, core: 2. Of those that a mesh axis runs over, the one named last changes fastest.
Arguments:
- kernel: float32 [16384, 16384], P('row', 'col'), may hold values from 0 to 9, as said below
Outputs:
- factored: float32 [16384, 16384], P('row', 'col')
The draws below stay inside these ranges and needn't reach their ends.
Inputs may be any that keep to these rules, and one draw needn't show every extreme that they name: `kernel`: ordered is symmetric and equals a positive semi-definite matrix plus a diagonal whose entries are 0.5 or more.
All inputs are finite; a program needn't handle non-finite values.
Results may differ from the reference program's by a relative error of at most 0.0003.
Values sent between devices are 32-bit elements; how exact they have to be, the bound alone decides.
No kernel may reach another device: no remote copies, remote signals or barrier semaphores. Data moves between devices by JAX's collectives and lax.ppermute only.
A program may use at most 128 MiB of HBM per device.

```python
import math
import jax
import jax.numpy as jnp
from jax import lax

NB = 256
PANELS = 3
M = 16384
N_ROW = 8
N_COL = 32


def stored_order(ordered):
    shaped = ordered.reshape(M // N_ROW // NB, N_ROW, NB, M // N_COL // NB, N_COL, NB)
    return shaped.transpose(1, 0, 2, 4, 3, 5).reshape(M, M)


def draw_kernel(key, part):
    key = jax.random.fold_in(key, 11)
    key_points, key_amplitude, key_jitter = jax.random.split(key, 3)
    points = 0.6 * jax.random.normal(key_points, (M, 8), jnp.float32)
    amplitude = jnp.exp(jax.random.uniform(key_amplitude, (M,), jnp.float32, math.log(0.5), math.log(2.0)))
    jitter = jax.random.uniform(key_jitter, (M,), jnp.float32, 0.5, 1.5)
    distance = jnp.zeros((M, M), jnp.float32)
    for axis_step in range(8):
        coord = points[:, axis_step]
        offset = coord[:, None] - coord[None, :]
        distance = distance + offset * offset
    matrix = amplitude[:, None] * amplitude[None, :] * jnp.exp(-0.5 * distance)
    places = jnp.arange(M)
    return stored_order(matrix.at[places, places].add(jitter))


def setup_inputs(seed: int = 0) -> dict:
    key_of = jax.random.split(jax.random.key(seed), 2)
    kernel = draw_kernel(jax.random.fold_in(key_of[1], 71), 0)
    return dict(kernel=kernel)


def to_global(stored):
    shaped = stored.reshape(N_ROW, M // N_ROW // NB, NB, N_COL, M // N_COL // NB, NB)
    return shaped.transpose(1, 0, 2, 4, 3, 5).reshape(M, M)

def to_stored(ordered):
    shaped = ordered.reshape(M // N_ROW // NB, N_ROW, NB, M // N_COL // NB, N_COL, NB)
    return shaped.transpose(1, 0, 2, 4, 3, 5).reshape(M, M)

def reference(kernel):
    working = to_global(kernel)
    identity = jnp.eye(NB, dtype=jnp.float32)
    for panel_index in range(PANELS):
        start = panel_index * NB
        finish = start + NB
        diag_factor = jnp.tril(jnp.linalg.cholesky(working[start:finish, start:finish]))
        diag_inverse = lax.linalg.triangular_solve(diag_factor, identity, left_side=True, lower=True)
        panel = jnp.dot(working[finish:, start:finish], diag_inverse.T, precision=lax.Precision.HIGHEST)
        update = jnp.dot(panel, panel.T, precision=lax.Precision.HIGHEST)
        working = working.at[finish:, finish:].add(-update)
        column = jnp.concatenate([jnp.zeros((start, NB), jnp.float32), diag_factor, panel], axis=0)
        working = working.at[:, start:finish].set(column)
    block_count = M // NB
    tile_view = working.reshape(block_count, NB, block_count, NB)
    row_block = jnp.arange(block_count, dtype=jnp.int32)[:, None, None, None]
    col_block = jnp.arange(block_count, dtype=jnp.int32)[None, None, :, None]
    lowered = jnp.where(row_block >= col_block, tile_view, jnp.zeros_like(tile_view))
    return to_stored(lowered.reshape(M, M))
```

```python
import jax
import jax.numpy as jnp
from jax import lax
from jax.experimental import pallas as pl
from jax.experimental.pallas import tpu as pltpu
from jax.sharding import Mesh
from jax.sharding import PartitionSpec as P

NB = 256
PANELS = 3
LEAD = NB * PANELS
HALF = 128
F32 = jnp.float32
BF16 = jnp.bfloat16


def dot_full(left, right, left_dim, right_dim):
    return lax.dot_general(
        left,
        right,
        (((left_dim,), (right_dim,)), ((), ())),
        precision=lax.Precision.HIGHEST,
        preferred_element_type=F32,
    )


def split(value):
    high = value.astype(BF16)
    return high, (value - high.astype(F32)).astype(BF16)


def row_of(value, step):
    return jnp.broadcast_to(value[step : step + 1], value.shape)


def inverse_factor(block):
    groups = HALF // 8
    rows = lax.broadcasted_iota(jnp.int32, (8, HALF), 0)
    lanes = lax.broadcasted_iota(jnp.int32, (8, HALF), 1)
    left = [block[8 * g : 8 * g + 8] for g in range(groups)]
    right = [(lanes == rows + 8 * g).astype(F32) for g in range(groups)]
    for first in range(groups):
        columns = [
            [
                jnp.broadcast_to(left[g][:, 8 * first + j : 8 * first + j + 1], (8, HALF))
                if g >= first
                else None
                for g in range(groups)
            ]
            for j in range(8)
        ]
        pivots = rows.astype(F32)
        for j in range(8):
            pivot = row_of(columns[j][first], j)
            inverse = pl.reciprocal(pivot, approx=True)
            inverse = inverse * (2.0 - pivot * inverse)
            pivots = jnp.where(rows == j, pivot, pivots)
            left_row = row_of(left[first], j)
            right_row = row_of(right[first], j)
            heads = [row_of(columns[i][first], j) for i in range(j + 1, 8)]
            for g in range(first, groups):
                scale = columns[j][g] * inverse
                if g == first:
                    if j == 7:
                        continue
                    scale = jnp.where(rows > j, scale, 0.0)
                for i in range(j + 1, 8):
                    columns[i][g] = columns[i][g] - scale * heads[i - j - 1]
                left[g] = left[g] - scale * left_row
                right[g] = right[g] - scale * right_row
        right[first] = right[first] * lax.rsqrt(pivots)
    return jnp.concatenate(right, 0)


BLOCKS = [(k, j) for k in range(PANELS) for j in range(k + 1)]


def solve_kernel(place_ref, lead_ref, cols_ref, high_ref, low_ref, work, inv, rhs):
    my_col = place_ref[1]
    for slot, (k, j) in enumerate(BLOCKS):
        for z in range(8):
            for h in range(2):
                at = k * NB + z * 32 + h * 16
                work[at : at + 16, j * NB : (j + 1) * NB] = lead_ref[z, h, slot]
    rhs[...] = cols_ref[...]
    for p in range(2 * PANELS):
        here = slice(p * HALF, (p + 1) * HALF)
        inverse = inverse_factor(work[here, here])
        if p % 2 == 0:
            inv[here, 0:HALF] = inverse
            inv[here, HALF:NB] = jnp.zeros_like(inverse)
        else:
            before = slice((p - 1) * HALF, p * HALF)
            cross = dot_full(work[here, before], inv[before, 0:HALF], 1, 0)
            inv[here, 0:HALF] = -dot_full(inverse, cross, 1, 0)
            inv[here, HALF:NB] = inverse
        if p + 1 < 2 * PANELS:
            below = slice((p + 1) * HALF, LEAD)
            factor = dot_full(work[below, here], inverse, 1, 1)
            work[below, here] = factor
            work[below, below] = work[below, below] - dot_full(factor, factor, 1, 1)
    for p in range(PANELS):
        here = slice(p * NB, (p + 1) * NB)
        rhs[here] = dot_full(inv[here], rhs[here], 1, 0)
        if p + 1 < PANELS:
            below = slice((p + 1) * NB, LEAD)
            rhs[below] = rhs[below] - dot_full(work[below, here], rhs[here], 1, 0)

    @pl.when(my_col < PANELS)
    def _():
        rows = lax.broadcasted_iota(jnp.int32, (LEAD, NB), 0)
        lanes = lax.broadcasted_iota(jnp.int32, (LEAD, NB), 1)
        rhs[:, 0:NB] = (rows == lanes + my_col * NB).astype(F32)

    for p in reversed(range(PANELS)):
        here = slice(p * NB, (p + 1) * NB)
        solved = dot_full(inv[here].T, rhs[here], 1, 0)
        rhs[here] = solved
        if p > 0:
            above = slice(0, p * NB)
            rhs[above] = rhs[above] - dot_full(work[here, above].T, solved, 1, 0)
    high, low = split(rhs[...])
    high_ref[...] = high
    low_ref[...] = low


def solve_lead(place, lead, cols):
    width = cols.shape[1]
    vmem = pl.BlockSpec(memory_space=pltpu.VMEM)
    return pl.pallas_call(
        solve_kernel,
        out_shape=[jax.ShapeDtypeStruct((LEAD, width), BF16)] * 2,
        in_specs=[pl.BlockSpec(memory_space=pltpu.SMEM), vmem, vmem],
        out_specs=[vmem, vmem],
        scratch_shapes=[
            pltpu.VMEM((LEAD, LEAD), F32),
            pltpu.VMEM((LEAD, NB), F32),
            pltpu.VMEM((LEAD, width), F32),
        ],
        compiler_params=pltpu.CompilerParams(vmem_limit_bytes=40 * 2**20),
        cost_estimate=pl.CostEstimate(flops=20 * 10**9, bytes_accessed=6 * 2**20, transcendentals=0),
        name="solve_lead",
    )(place, lead, cols)


def update_kernel(place_ref, base_ref, rows_ref, high_ref, low_ref, out_ref):
    step = pl.program_id(0)
    row_id = place_ref[0] + place_ref[2] * step
    for half in range(2):
        col_id = place_ref[1] + place_ref[3] * half
        span = slice(half * NB, (half + 1) * NB)

        @pl.when(row_id < col_id)
        def _():
            out_ref[:, span] = jnp.zeros((NB, NB), F32)

        @pl.when(row_id >= col_id)
        def _():
            total = jnp.zeros((NB, NB), F32)
            for k in range(PANELS):
                inner = slice(k * NB, (k + 1) * NB)
                high, low = split(rows_ref[0, :, k].reshape(NB, NB))
                for left, right in ((low, high_ref), (high, low_ref), (high, high_ref)):
                    total = total + jnp.dot(left, right[inner, span], preferred_element_type=F32)
            panel = col_id < PANELS

            @pl.when(panel)
            def _():
                rows = lax.broadcasted_iota(jnp.int32, (NB, NB), 0)
                lanes = lax.broadcasted_iota(jnp.int32, (NB, NB), 1)
                keep = (rows >= lanes) | (row_id > col_id)
                out_ref[:, span] = jnp.where(keep, total, 0.0)

            @pl.when(jnp.logical_not(panel))
            def _():
                out_ref[:, span] = base_ref[:, span] - total


def update(place, base, gathered, high, low):
    rows, width = base.shape
    steps = rows // NB
    return pl.pallas_call(
        update_kernel,
        grid=(steps,),
        out_shape=jax.ShapeDtypeStruct(base.shape, F32),
        in_specs=[
            pl.BlockSpec(memory_space=pltpu.SMEM),
            pl.BlockSpec((NB, width), lambda a: (a, 0)),
            pl.BlockSpec((1, 4, PANELS, 64, NB), lambda a: (a % 4, a // 4, 0, 0, 0)),
            pl.BlockSpec(memory_space=pltpu.VMEM),
            pl.BlockSpec(memory_space=pltpu.VMEM),
        ],
        out_specs=pl.BlockSpec((NB, width), lambda a: (a, 0)),
        compiler_params=pltpu.CompilerParams(vmem_limit_bytes=40 * 2**20),
        cost_estimate=pl.CostEstimate(flops=5 * 10**9, bytes_accessed=16 * 2**20, transcendentals=0),
        name="update",
    )(place, base, gathered, high, low)


N_X, N_CORE, N_Y, N_Z = 4, 2, 4, 8
N_ROW = N_X * N_CORE
N_COL = N_Y * N_Z
AXES = ("x", "core", "y", "z")
PIECE = NB // N_Z


def device(row, y, z):
    return (row * N_Y + y) * N_Z + z


def send(value, pairs):
    return lax.ppermute(value, AXES, pairs)


def pick(stacked, index):
    return lax.dynamic_index_in_dim(stacked, index % stacked.shape[0], 0, keepdims=False)


def share_rows(strip, my_row, my_y, my_z):
    pieces = strip.T.reshape(N_Z, 2 * NB // N_Z, NB)
    received = []
    for step in range(N_Z):
        pairs = [
            (device(k, y, z), device(z, y, (z + step + k) % N_Z))
            for k in range(PANELS)
            for y in range(N_Y)
            for z in range(N_Z)
        ]
        received.append(send(pick(pieces, my_z + step + my_row), pairs))
    received = jnp.stack(received)
    mine = jnp.stack([pick(received, my_z - my_row - k) for k in range(PANELS)])
    return lax.all_gather(mine, ("y", "z")).reshape(N_Y, N_Z, PANELS, 2 * NB // N_Z, NB)


def share_lead(strip, my_row, my_core, my_y, my_z):
    pieces = strip[:, 0:NB].reshape(N_Z, PIECE, NB)
    received = [pick(pieces, my_z)]
    for step in range(1, N_Z):
        pairs = [
            (device(k, 0, j), device(k, 0, (j + step) % N_Z)) for k in range(PANELS) for j in range(k + 1)
        ]
        received.append(send(pick(pieces, my_z + step), pairs))
    received = jnp.stack(received)
    spread = jnp.stack([pick(received, my_z - j) for j in range(PANELS)])
    others = [
        send(spread, [(device(k, 0, z), device(k, y, z)) for k in range(PANELS) for z in range(N_Z)])
        for y in range(1, N_Y)
    ]
    spread = jnp.where(my_y == 0, spread, others[0] + others[1] + others[2])
    halves = spread.reshape(PANELS, N_CORE, PIECE // N_CORE, NB).transpose(1, 0, 2, 3)
    received = [pick(halves, my_core)]
    for step in range(1, N_ROW):
        pairs = [
            (device(k, y, z), device((k + step) % N_ROW, y, z))
            for k in range(PANELS)
            for y in range(N_Y)
            for z in range(N_Z)
        ]
        received.append(send(pick(halves, my_row + step), pairs))
    received = jnp.stack(received)
    rows = [pick(received, my_row - k) for k in range(PANELS)]
    mine = jnp.stack([rows[k][j] for k, j in BLOCKS])
    around = [mine] + [
        lax.ppermute(mine, "z", [(z, (z + step) % N_Z) for z in range(N_Z)]) for step in range(1, N_Z)
    ]
    around = jnp.stack(around)
    half = jnp.stack([pick(around, my_z - z) for z in range(N_Z)])
    other = lax.ppermute(half, "core", [(0, 1), (1, 0)])
    first = jnp.where(my_core == 0, half, other)
    second = jnp.where(my_core == 0, other, half)
    return jnp.stack([first, second], axis=1)


def share_cols(strip, my_x, my_core):
    def pairs(moves):
        return [
            (device(2 * a + core, y, z), device(2 * b + core, y, z))
            for a, b, cores in moves
            for core in range(cores)
            for y in range(N_Y)
            for z in range(N_Z)
        ]

    up = send(strip, pairs([(0, 1, 2), (1, 2, 1)]))
    down = send(strip, pairs([(0, 3, 2), (1, 0, 1)]))
    onward = send(up, pairs([(1, 2, 2), (2, 3, 1)]))
    own = jnp.where(my_x == 0, strip, jnp.where(my_x == 1, up, jnp.where(my_x == 2, onward, down)))
    last = jnp.where(my_x == 0, down, jnp.where(my_x == 1, strip, jnp.where(my_x == 2, up, onward)))
    other = lax.ppermute(own, "core", [(0, 1), (1, 0)])
    passed = lax.ppermute(last, "core", [(0, 1)])
    first = jnp.where(my_core == 0, own, other)
    second = jnp.where(my_core == 0, other, own)
    last = jnp.where(my_core == 0, last, passed)
    return jnp.concatenate([first, second, last], axis=0)


def body(kernel):
    my_x, my_core = lax.axis_index("x"), lax.axis_index("core")
    my_y, my_z = lax.axis_index("y"), lax.axis_index("z")
    my_row = my_x * N_CORE + my_core
    my_col = my_y * N_Z + my_z
    place = jnp.stack([my_row, my_col, jnp.int32(N_ROW), jnp.int32(N_COL)]).astype(jnp.int32)
    strip = kernel[0:NB]
    gathered = share_rows(strip, my_row, my_y, my_z)
    lead = share_lead(strip, my_row, my_core, my_y, my_z)
    cols = share_cols(strip, my_x, my_core)
    high, low = solve_lead(place, lead, cols)
    return update(place, kernel, gathered, high, low)


def solution(mesh):
    fine = Mesh(mesh.devices.reshape(N_X, N_CORE, N_Y, N_Z), AXES)
    placed = P(("x", "core"), ("y", "z"))
    return jax.shard_map(body, mesh=fine, in_specs=(placed,), out_specs=placed, check_vma=False)
```

```python
import jax
import jax.numpy as jnp
from jax import lax
from jax.experimental import pallas as pl
from jax.experimental.pallas import tpu as pltpu
from jax.sharding import Mesh
from jax.sharding import PartitionSpec as P

NB = 256
PANELS = 3
LEAD = NB * PANELS
HALF = 128
F32 = jnp.float32
BF16 = jnp.bfloat16


def split(value):
    high = value.astype(BF16)
    return high, (value - high.astype(F32)).astype(BF16)


def dot_split(left, right, left_dim, right_dim):
    left_high, left_low = split(left)
    right_high, right_low = split(right)

    def dot(a, b):
        return lax.dot_general(a, b, (((left_dim,), (right_dim,)), ((), ())), preferred_element_type=F32)

    return dot(left_low, right_high) + dot(left_high, right_low) + dot(left_high, right_high)


def row_of(value, step):
    return jnp.broadcast_to(value[step : step + 1], value.shape)


def inverse_factor(block):
    groups = HALF // 8
    rows = lax.broadcasted_iota(jnp.int32, (8, HALF), 0)
    lanes = lax.broadcasted_iota(jnp.int32, (8, HALF), 1)
    left = [block[8 * g : 8 * g + 8] for g in range(groups)]
    right = [(lanes == rows + 8 * g).astype(F32) for g in range(groups)]
    for first in range(groups):
        columns = [
            [
                jnp.broadcast_to(left[g][:, 8 * first + j : 8 * first + j + 1], (8, HALF))
                if g >= first
                else None
                for g in range(groups)
            ]
            for j in range(8)
        ]
        pivots = rows.astype(F32)
        for j in range(8):
            pivot = row_of(columns[j][first], j)
            inverse = pl.reciprocal(pivot, approx=True)
            inverse = inverse * (2.0 - pivot * inverse)
            pivots = jnp.where(rows == j, pivot, pivots)
            left_row = row_of(left[first], j)
            right_row = row_of(right[first], j)
            heads = [row_of(columns[i][first], j) for i in range(j + 1, 8)]
            for g in range(first, groups):
                scale = columns[j][g] * inverse
                if g == first:
                    if j == 7:
                        continue
                    scale = jnp.where(rows > j, scale, 0.0)
                for i in range(j + 1, 8):
                    columns[i][g] = columns[i][g] - scale * heads[i - j - 1]
                left[g] = left[g] - scale * left_row
                right[g] = right[g] - scale * right_row
        right[first] = right[first] * lax.rsqrt(pivots)
    return jnp.concatenate(right, 0)


BLOCKS = [(k, j) for k in range(PANELS) for j in range(k + 1)]


def factor_kernel(lead_ref, work, inv):
    for slot, (k, j) in enumerate(BLOCKS):
        for r in range(8):
            at = k * NB + r * PIECE
            work[at : at + PIECE, j * NB : (j + 1) * NB] = lead_ref[r, slot]

    @pl.loop(0, 2 * PANELS)
    def _(p):
        at = pl.multiple_of(p * HALF, HALF)
        inverse = inverse_factor(work[pl.ds(at, HALF), pl.ds(at, HALF)])

        @pl.when(p % 2 == 0)
        def _():
            inv[pl.ds(at, HALF), 0:HALF] = inverse
            inv[pl.ds(at, HALF), HALF:NB] = jnp.zeros_like(inverse)

        @pl.when(p % 2 == 1)
        def _():
            before = pl.multiple_of((p - 1) * HALF, HALF)
            cross = dot_split(work[pl.ds(at, HALF), pl.ds(before, HALF)], inv[pl.ds(before, HALF), 0:HALF], 1, 0)
            inv[pl.ds(at, HALF), 0:HALF] = -dot_split(inverse, cross, 1, 0)
            inv[pl.ds(at, HALF), HALF:NB] = inverse

        for done in range(2 * PANELS - 1):

            @pl.when(p == done)
            def _():
                here = slice(done * HALF, (done + 1) * HALF)
                below = slice((done + 1) * HALF, LEAD)
                factor = dot_split(work[below, here], inverse, 1, 1)
                work[below, here] = factor
                work[below, below] = work[below, below] - dot_split(factor, factor, 1, 1)


def factor_lead(lead):
    vmem = pl.BlockSpec(memory_space=pltpu.VMEM)
    return pl.pallas_call(
        factor_kernel,
        out_shape=[jax.ShapeDtypeStruct((LEAD, LEAD), F32), jax.ShapeDtypeStruct((LEAD, NB), F32)],
        in_specs=[vmem],
        out_specs=[vmem, vmem],
        compiler_params=pltpu.CompilerParams(vmem_limit_bytes=24 * 2**20),
        cost_estimate=pl.CostEstimate(flops=20 * 10**9, bytes_accessed=6 * 2**20, transcendentals=0),
        name="factor_lead",
    )(lead)


def solve_kernel(place_ref, work, inv, cols_ref, high_ref, low_ref, rhs):
    my_col = place_ref[1]
    rhs[...] = cols_ref[...]
    for p in range(PANELS):
        here = slice(p * NB, (p + 1) * NB)
        rhs[here] = dot_split(inv[here], rhs[here], 1, 0)
        if p + 1 < PANELS:
            below = slice((p + 1) * NB, LEAD)
            rhs[below] = rhs[below] - dot_split(work[below, here], rhs[here], 1, 0)

    @pl.when(my_col < PANELS)
    def _():
        rows = lax.broadcasted_iota(jnp.int32, (LEAD, NB), 0)
        lanes = lax.broadcasted_iota(jnp.int32, (LEAD, NB), 1)
        rhs[:, 0:NB] = (rows == lanes + my_col * NB).astype(F32)

    for p in reversed(range(PANELS)):
        here = slice(p * NB, (p + 1) * NB)
        solved = dot_split(inv[here].T, rhs[here], 1, 0)
        rhs[here] = solved
        if p > 0:
            above = slice(0, p * NB)
            rhs[above] = rhs[above] - dot_split(work[here, above].T, solved, 1, 0)
    high, low = split(rhs[...])
    high_ref[...] = high
    low_ref[...] = low


def solve_lead(place, work, inv, cols):
    width = cols.shape[1]
    vmem = pl.BlockSpec(memory_space=pltpu.VMEM)
    return pl.pallas_call(
        solve_kernel,
        out_shape=[jax.ShapeDtypeStruct((LEAD, width), BF16)] * 2,
        in_specs=[pl.BlockSpec(memory_space=pltpu.SMEM), vmem, vmem, vmem],
        out_specs=[vmem, vmem],
        scratch_shapes=[pltpu.VMEM((LEAD, width), F32)],
        compiler_params=pltpu.CompilerParams(vmem_limit_bytes=24 * 2**20),
        cost_estimate=pl.CostEstimate(flops=8 * 10**9, bytes_accessed=6 * 2**20, transcendentals=0),
        name="solve_lead",
    )(place, work, inv, cols)


def update_kernel(place_ref, base_ref, rows_ref, high_ref, low_ref, out_ref):
    first_id = place_ref[0] + place_ref[2] * pl.program_id(0)
    near = place_ref[1]
    left = slice(0, NB)
    right = slice(NB, 2 * NB)
    panel = near < PANELS

    def product(rows, span):
        parts = [split(rows_ref[0, rows, k].reshape(-1, NB)) for k in range(PANELS)]
        high = jnp.concatenate([part[0] for part in parts], axis=1)
        low = jnp.concatenate([part[1] for part in parts], axis=1)
        total = jnp.dot(low, high_ref[:, span], preferred_element_type=F32)
        total = total + jnp.dot(high, low_ref[:, span], preferred_element_type=F32)
        return total + jnp.dot(high, high_ref[:, span], preferred_element_type=F32)

    @pl.when(first_id >= near)
    def _():
        total = product(slice(0, 8), left).reshape(2, NB, NB)

        @pl.when(panel)
        def _():
            rows = lax.broadcasted_iota(jnp.int32, (NB, NB), 0)
            lanes = lax.broadcasted_iota(jnp.int32, (NB, NB), 1)
            out_ref[0, :, left] = jnp.where((rows >= lanes) | (first_id > near), total[0], 0.0)
            out_ref[1, :, left] = total[1]

        @pl.when(jnp.logical_not(panel))
        def _():
            out_ref[:, :, left] = base_ref[:, :, left] - total

        out_ref[0, :, right] = jnp.zeros((NB, NB), F32)
        out_ref[1, :, right] = base_ref[1, :, right] - product(slice(4, 8), right)

    @pl.when(first_id < near)
    def _():
        out_ref[0] = jnp.zeros((NB, 2 * NB), F32)
        total = product(slice(4, 8), left)
        out_ref[1, :, left] = jnp.where(panel, total, base_ref[1, :, left] - total)
        out_ref[1, :, right] = jnp.zeros((NB, NB), F32)


def update(place, base, gathered, high, low):
    rows, width = base.shape
    pairs = base.reshape(2, rows // 2, width)
    return pl.pallas_call(
        update_kernel,
        grid=(rows // NB // 2,),
        out_shape=jax.ShapeDtypeStruct(pairs.shape, F32),
        in_specs=[
            pl.BlockSpec(memory_space=pltpu.SMEM),
            pl.BlockSpec((2, NB, width), lambda y: (0, y, 0)),
            pl.BlockSpec((1, 8, PANELS, 64, NB), lambda y: (y, 0, 0, 0, 0)),
            pl.BlockSpec(memory_space=pltpu.VMEM),
            pl.BlockSpec(memory_space=pltpu.VMEM),
        ],
        out_specs=pl.BlockSpec((2, NB, width), lambda y: (0, y, 0)),
        compiler_params=pltpu.CompilerParams(vmem_limit_bytes=57 * 2**20),
        cost_estimate=pl.CostEstimate(flops=5 * 10**9, bytes_accessed=16 * 2**20, transcendentals=0),
        name="update",
    )(place, pairs, gathered, high, low).reshape(rows, width)


N_X, N_CORE, N_Y, N_Z = 4, 2, 4, 8
N_ROW = N_X * N_CORE
N_COL = N_Y * N_Z
AXES = ("x", "core", "y", "z")
PIECE = NB // N_Z


def device(row, y, z):
    return (row * N_Y + y) * N_Z + z


def send(value, pairs):
    return lax.ppermute(value, AXES, pairs)


def pick(stacked, index):
    return lax.dynamic_index_in_dim(stacked, index % stacked.shape[0], 0, keepdims=False)


def scatter_rows(strip, my_row, my_y, my_z):
    pieces = strip.T.reshape(N_Z, 2 * NB // N_Z, NB)
    received = []
    for step in range(N_Z):
        pairs = [
            (device(k, y, z), device(z, y, (z + step + k) % N_Z))
            for k in range(PANELS)
            for y in range(N_Y)
            for z in range(N_Z)
        ]
        received.append(send(pick(pieces, my_z + step + my_row), pairs))
    received = jnp.stack(received)
    return jnp.stack([pick(received, my_z - my_row - k) for k in range(PANELS)])


def scatter_lead(strip, my_x, my_core):
    pieces = strip[:, 0:NB].reshape(N_X, N_CORE, PIECE, NB)
    keep = lax.dynamic_index_in_dim(pieces, my_core, 1, keepdims=False)
    give = lax.dynamic_index_in_dim(pieces, 1 - my_core, 1, keepdims=False)
    got = lax.ppermute(give, "core", [(0, 1), (1, 0)])
    both = jnp.stack(
        [jnp.where(my_core == 0, keep, got), jnp.where(my_core == 0, got, keep)], axis=1
    )
    received = [pick(both, my_x)]
    for step in range(1, N_X):
        pairs = [
            (device(N_CORE * x + core, 0, j), device(N_CORE * ((x + step) % N_X) + core, 0, j))
            for x in range(2)
            for core in range(N_CORE)
            for j in range(PANELS)
        ]
        received.append(send(pick(both, my_x + step), pairs))
    received = jnp.stack(received)
    return jnp.concatenate([pick(received, my_x), pick(received, my_x - 1)[0:1]], axis=0)


def spread_lead(parts, my_z):
    far = send(
        parts, [(device(r, 0, j), device(r, 0, j + N_Z // 2)) for r in range(N_ROW) for j in range(PANELS)]
    )
    hold = jnp.where(my_z >= N_Z // 2, far, parts)
    received = [hold]
    for step in range(1, N_Z // 2):
        pairs = [
            (device(r, 0, j + half), device(r, 0, (j + half + step) % N_Z))
            for r in range(N_ROW)
            for j in range(PANELS)
            for half in (0, N_Z // 2)
        ]
        received.append(send(hold, pairs))
    received = jnp.stack(received)
    spread = [pick(received, my_z - j) for j in range(PANELS)]
    return jnp.stack([spread[j][k] for k, j in BLOCKS])


def share_lead(mine, my_x, my_y):
    others = [
        send(mine, [(device(r, 0, z), device(r, y, z)) for r in range(N_ROW) for z in range(N_Z)])
        for y in range(1, N_Y)
    ]
    mine = jnp.where(my_y == 0, mine, others[0] + others[1] + others[2])
    around = [mine] + [
        lax.ppermute(mine, "x", [(x, (x + step) % N_X) for x in range(N_X)]) for step in range(1, N_X)
    ]
    around = jnp.stack(around)
    return jnp.stack([pick(around, my_x - x) for x in range(N_X)])


def swap_lead(half, my_core):
    other = lax.ppermute(half, "core", [(0, 1), (1, 0)])
    first = jnp.where(my_core == 0, half, other)
    second = jnp.where(my_core == 0, other, half)
    return jnp.stack([first, second], axis=1).reshape(N_ROW, len(BLOCKS), PIECE, NB)


def col_pairs(moves):
    return [
        (device(2 * a + core, y, z), device(2 * b + core, y, z))
        for a, b, cores in moves
        for core in range(cores)
        for y in range(N_Y)
        for z in range(N_Z)
    ]


def cols_out(strip):
    return send(strip, col_pairs([(0, 1, 2), (1, 2, 1)])), send(strip, col_pairs([(0, 3, 2), (1, 0, 1)]))


def cols_on(up):
    return send(up, col_pairs([(1, 2, 2), (2, 3, 1)]))


def swap_cols(strip, up, down, onward, my_x, my_core):
    own = jnp.where(my_x == 0, strip, jnp.where(my_x == 1, up, jnp.where(my_x == 2, onward, down)))
    last = jnp.where(my_x == 0, down, jnp.where(my_x == 1, strip, jnp.where(my_x == 2, up, onward)))
    other = lax.ppermute(own, "core", [(0, 1), (1, 0)])
    passed = lax.ppermute(last, "core", [(0, 1)])
    first = jnp.where(my_core == 0, own, other)
    second = jnp.where(my_core == 0, other, own)
    last = jnp.where(my_core == 0, last, passed)
    return jnp.concatenate([first, second, last], axis=0)


def body(kernel):
    my_x, my_core = lax.axis_index("x"), lax.axis_index("core")
    my_y, my_z = lax.axis_index("y"), lax.axis_index("z")
    my_row = my_x * N_CORE + my_core
    my_col = my_y * N_Z + my_z
    place = jnp.stack([my_row, my_col, jnp.int32(N_ROW), jnp.int32(N_COL)]).astype(jnp.int32)
    strip = kernel[0:NB]
    parts = scatter_lead(strip, my_x, my_core)
    strip, parts = lax.optimization_barrier((strip, parts))
    mine = scatter_rows(strip, my_row, my_y, my_z)
    eighth = spread_lead(parts, my_z)
    strip, mine = lax.optimization_barrier((strip, mine))
    gathered = lax.all_gather(mine, ("y", "z")).reshape(N_Y, N_Z, PANELS, 2 * NB // N_Z, NB)
    up, down = cols_out(strip)
    eighth, up, down = lax.optimization_barrier((eighth, up, down))
    onward = cols_on(up)
    quarter = share_lead(eighth, my_x, my_y)
    quarter, onward = lax.optimization_barrier((quarter, onward))
    lead = swap_lead(quarter, my_core)
    cols = swap_cols(strip, up, down, onward, my_x, my_core)
    work, inv = factor_lead(lead)
    high, low = solve_lead(place, work, inv, cols)
    return update(place, kernel, gathered, high, low)


def solution(mesh):
    fine = Mesh(mesh.devices.reshape(N_X, N_CORE, N_Y, N_Z), AXES)
    placed = P(("x", "core"), ("y", "z"))
    return jax.shard_map(body, mesh=fine, in_specs=(placed,), out_specs=placed, check_vma=False)
```

```python
import jax
import jax.numpy as jnp
from jax import lax
from jax.experimental import pallas as pl
from jax.experimental.pallas import tpu as pltpu
from jax.sharding import Mesh
from jax.sharding import PartitionSpec as P

NB = 256
PANELS = 3
LEAD = NB * PANELS
HALF = 128
F32 = jnp.float32
BF16 = jnp.bfloat16


def split(value):
    high = value.astype(BF16)
    return high, (value - high.astype(F32)).astype(BF16)


def dot_split(left, right, left_dim, right_dim):
    left_high, left_low = split(left)
    right_high, right_low = split(right)

    def dot(a, b):
        return lax.dot_general(a, b, (((left_dim,), (right_dim,)), ((), ())), preferred_element_type=F32)

    return dot(left_low, right_high) + dot(left_high, right_low) + dot(left_high, right_high)


def row_of(value, step):
    return jnp.take_along_axis(value, jnp.full(value.shape, step, jnp.int32), axis=0)


def inverse_factor(block):
    groups = HALF // 8
    rows = lax.broadcasted_iota(jnp.int32, (8, HALF), 0)
    lanes = lax.broadcasted_iota(jnp.int32, (8, HALF), 1)
    left = [block[8 * g : 8 * g + 8] for g in range(groups)]
    right = [(lanes == rows + 8 * g).astype(F32) for g in range(groups)]
    for first in range(groups):
        columns = [
            [
                jnp.broadcast_to(left[g][:, 8 * first + j : 8 * first + j + 1], (8, HALF))
                if g >= first
                else None
                for g in range(groups)
            ]
            for j in range(8)
        ]
        pivots = rows.astype(F32)
        for j in range(8):
            pivot = row_of(columns[j][first], j)
            inverse = pl.reciprocal(pivot, approx=True)
            inverse = inverse * (2.0 - pivot * inverse)
            pivots = jnp.where(rows == j, pivot, pivots)
            left_row = row_of(left[first], j)
            right_row = row_of(right[first], j)
            heads = [row_of(columns[i][first], j) for i in range(j + 1, 8)]
            for g in range(first, groups):
                scale = columns[j][g] * inverse
                if g == first:
                    if j == 7:
                        continue
                    scale = jnp.where(rows > j, scale, 0.0)
                for i in range(j + 1, 8):
                    columns[i][g] = columns[i][g] - scale * heads[i - j - 1]
                left[g] = left[g] - scale * left_row
                right[g] = right[g] - scale * right_row
        right[first] = right[first] * lax.rsqrt(pivots)
    return jnp.concatenate(right, 0)


BLOCKS = [(j, j) for j in range(PANELS)] + [((j + 1) % PANELS, j) for j in range(PANELS)]


def factor_kernel(lead_ref, work, inv):
    for slot, (k, j) in enumerate(BLOCKS):
        if k >= j:
            for r in range(8):
                at = k * NB + r * PIECE
                work[at : at + PIECE, j * NB : (j + 1) * NB] = lead_ref[r, slot]
        else:
            turned = lead_ref[:, slot].reshape(NB, NB).T
            work[j * NB : (j + 1) * NB, k * NB : (k + 1) * NB] = turned

    @pl.loop(0, 2 * PANELS)
    def _(p):
        at = pl.multiple_of(p * HALF, HALF)
        inverse = inverse_factor(work[pl.ds(at, HALF), pl.ds(at, HALF)])

        @pl.when(p % 2 == 0)
        def _():
            inv[pl.ds(at, HALF), 0:HALF] = inverse
            inv[pl.ds(at, HALF), HALF:NB] = jnp.zeros_like(inverse)

        @pl.when(p % 2 == 1)
        def _():
            before = pl.multiple_of((p - 1) * HALF, HALF)
            cross = dot_split(work[pl.ds(at, HALF), pl.ds(before, HALF)], inv[pl.ds(before, HALF), 0:HALF], 1, 0)
            inv[pl.ds(at, HALF), 0:HALF] = -dot_split(inverse, cross, 1, 0)
            inv[pl.ds(at, HALF), HALF:NB] = inverse

        for done in range(2 * PANELS - 1):

            @pl.when(p == done)
            def _():
                here = slice(done * HALF, (done + 1) * HALF)
                below = slice((done + 1) * HALF, LEAD)
                factor = dot_split(work[below, here], inverse, 1, 1)
                work[below, here] = factor
                work[below, below] = work[below, below] - dot_split(factor, factor, 1, 1)


def factor_lead(lead):
    vmem = pl.BlockSpec(memory_space=pltpu.VMEM)
    return pl.pallas_call(
        factor_kernel,
        out_shape=[jax.ShapeDtypeStruct((LEAD, LEAD), F32), jax.ShapeDtypeStruct((LEAD, NB), F32)],
        in_specs=[vmem],
        out_specs=[vmem, vmem],
        compiler_params=pltpu.CompilerParams(vmem_limit_bytes=24 * 2**20),
        cost_estimate=pl.CostEstimate(flops=20 * 10**9, bytes_accessed=6 * 2**20, transcendentals=0),
        name="factor_lead",
    )(lead)


def solve_kernel(place_ref, work, inv, cols_ref, high_ref, low_ref, rhs):
    my_col = place_ref[1]
    rhs[...] = cols_ref[...]
    for p in range(PANELS):
        here = slice(p * NB, (p + 1) * NB)
        rhs[here] = dot_split(inv[here], rhs[here], 1, 0)
        if p + 1 < PANELS:
            below = slice((p + 1) * NB, LEAD)
            rhs[below] = rhs[below] - dot_split(work[below, here], rhs[here], 1, 0)

    @pl.when(my_col < PANELS)
    def _():
        rows = lax.broadcasted_iota(jnp.int32, (LEAD, NB), 0)
        lanes = lax.broadcasted_iota(jnp.int32, (LEAD, NB), 1)
        rhs[:, 0:NB] = (rows == lanes + my_col * NB).astype(F32)

    for p in reversed(range(PANELS)):
        here = slice(p * NB, (p + 1) * NB)
        solved = dot_split(inv[here].T, rhs[here], 1, 0)
        rhs[here] = solved
        if p > 0:
            above = slice(0, p * NB)
            rhs[above] = rhs[above] - dot_split(work[here, above].T, solved, 1, 0)
    high, low = split(rhs[...])
    high_ref[...] = high
    low_ref[...] = low


def solve_lead(place, work, inv, cols):
    width = cols.shape[1]
    vmem = pl.BlockSpec(memory_space=pltpu.VMEM)
    return pl.pallas_call(
        solve_kernel,
        out_shape=[jax.ShapeDtypeStruct((LEAD, width), BF16)] * 2,
        in_specs=[pl.BlockSpec(memory_space=pltpu.SMEM), vmem, vmem, vmem],
        out_specs=[vmem, vmem],
        scratch_shapes=[pltpu.VMEM((LEAD, width), F32)],
        compiler_params=pltpu.CompilerParams(vmem_limit_bytes=24 * 2**20),
        cost_estimate=pl.CostEstimate(flops=8 * 10**9, bytes_accessed=6 * 2**20, transcendentals=0),
        name="solve_lead",
    )(place, work, inv, cols)


def update_kernel(place_ref, base_ref, rows_ref, high_ref, low_ref, out_ref):
    first_id = place_ref[0] + place_ref[2] * pl.program_id(0)
    near = place_ref[1]
    left = slice(0, NB)
    right = slice(NB, 2 * NB)
    panel = near < PANELS

    def product(rows, span):
        parts = [split(rows_ref[0, rows, k].reshape(-1, NB)) for k in range(PANELS)]
        high = jnp.concatenate([part[0] for part in parts], axis=1)
        low = jnp.concatenate([part[1] for part in parts], axis=1)
        outs = []
        for at in range(0, high.shape[0], HALF):
            some = slice(at, at + HALF)
            total = jnp.dot(low[some], high_ref[:, span], preferred_element_type=F32)
            total = total + jnp.dot(high[some], low_ref[:, span], preferred_element_type=F32)
            outs.append(total + jnp.dot(high[some], high_ref[:, span], preferred_element_type=F32))
        return jnp.concatenate(outs, axis=0)

    @pl.when(first_id >= near)
    def _():
        total = product(slice(0, 8), left).reshape(2, NB, NB)

        @pl.when(panel)
        def _():
            rows = lax.broadcasted_iota(jnp.int32, (NB, NB), 0)
            lanes = lax.broadcasted_iota(jnp.int32, (NB, NB), 1)
            out_ref[0, :, left] = jnp.where((rows >= lanes) | (first_id > near), total[0], 0.0)
            out_ref[1, :, left] = total[1]

        @pl.when(jnp.logical_not(panel))
        def _():
            out_ref[:, :, left] = base_ref[:, :, left] - total

        out_ref[0, :, right] = jnp.zeros((NB, NB), F32)
        out_ref[1, :, right] = base_ref[1, :, right] - product(slice(4, 8), right)

    @pl.when(first_id < near)
    def _():
        out_ref[0] = jnp.zeros((NB, 2 * NB), F32)
        total = product(slice(4, 8), left)
        out_ref[1, :, left] = jnp.where(panel, total, base_ref[1, :, left] - total)
        out_ref[1, :, right] = jnp.zeros((NB, NB), F32)


def update(place, base, gathered, high, low):
    rows, width = base.shape
    pairs = base.reshape(2, rows // 2, width)
    return pl.pallas_call(
        update_kernel,
        grid=(rows // NB // 2,),
        out_shape=jax.ShapeDtypeStruct(pairs.shape, F32),
        in_specs=[
            pl.BlockSpec(memory_space=pltpu.SMEM),
            pl.BlockSpec((2, NB, width), lambda y: (0, y, 0)),
            pl.BlockSpec((1, 8, PANELS, 64, NB), lambda y: (y, 0, 0, 0, 0)),
            pl.BlockSpec(memory_space=pltpu.VMEM),
            pl.BlockSpec(memory_space=pltpu.VMEM),
        ],
        out_specs=pl.BlockSpec((2, NB, width), lambda y: (0, y, 0)),
        compiler_params=pltpu.CompilerParams(vmem_limit_bytes=50 * 2**20),
        cost_estimate=pl.CostEstimate(flops=5 * 10**9, bytes_accessed=16 * 2**20, transcendentals=0),
        name="update",
    )(place, pairs, gathered, high, low).reshape(rows, width)


N_X, N_CORE, N_Y, N_Z = 4, 2, 4, 8
N_ROW = N_X * N_CORE
N_COL = N_Y * N_Z
AXES = ("x", "core", "y", "z")
PIECE = NB // N_Z


def device(row, y, z):
    return (row * N_Y + y) * N_Z + z


def send(value, pairs):
    return lax.ppermute(value, AXES, pairs)


def pick(stacked, index):
    return lax.dynamic_index_in_dim(stacked, index % stacked.shape[0], 0, keepdims=False)


def scatter_rows(strip, my_row, my_y, my_z):
    pieces = strip.T.reshape(N_Z, 2 * NB // N_Z, NB)
    received = []
    for step in range(N_Z):
        pairs = [
            (device(k, y, z), device(z, y, (z + step + k) % N_Z))
            for k in range(PANELS)
            for y in range(N_Y)
            for z in range(N_Z)
        ]
        received.append(send(pick(pieces, my_z + step + my_row), pairs))
    received = jnp.stack(received)
    return jnp.stack([pick(received, my_z - my_row - k) for k in range(PANELS)])


def scatter_lead(strip, my_x, my_core, my_z):
    pieces = strip[:, 0:NB].reshape(N_X, N_CORE, PIECE, NB)
    keep = lax.dynamic_index_in_dim(pieces, my_core, 1, keepdims=False)
    give = lax.dynamic_index_in_dim(pieces, 1 - my_core, 1, keepdims=False)
    got = lax.ppermute(give, "core", [(0, 1), (1, 0)])
    both = jnp.stack(
        [jnp.where(my_core == 0, keep, got), jnp.where(my_core == 0, got, keep)], axis=1
    )
    received = [pick(both, my_x)]
    for step in range(1, N_X):
        pairs = [
            (device(N_CORE * x + core, 0, j), device(N_CORE * ((x + step) % N_X) + core, 0, j))
            for x in range(2)
            for core in range(N_CORE)
            for j in range(PANELS)
        ]
        received.append(send(pick(both, my_x + step), pairs))
    received = jnp.stack(received)
    parts = jnp.concatenate([pick(received, my_x), pick(received, my_x - 1)[0:1]], axis=0)
    return jnp.stack([pick(parts, my_z), pick(parts, my_z + 1)])


def spread_lead(parts, my_z):
    far = send(
        parts, [(device(r, 0, j), device(r, 0, j + N_Z // 2)) for r in range(N_ROW) for j in range(PANELS)]
    )
    hold = jnp.where(my_z >= N_Z // 2, far, parts)
    received = [hold]
    for step in range(1, N_Z // 2):
        pairs = [
            (device(r, 0, j + half), device(r, 0, (j + half + step) % N_Z))
            for r in range(N_ROW)
            for j in range(PANELS)
            for half in (0, N_Z // 2)
        ]
        received.append(send(hold, pairs))
    received = jnp.stack(received)
    spread = [pick(received, my_z - j) for j in range(PANELS)]
    return jnp.stack(spread, axis=1).reshape(len(BLOCKS), PIECE, NB)


def share_lead(mine, my_x, my_y):
    others = [
        send(mine, [(device(r, 0, z), device(r, y, z)) for r in range(N_ROW) for z in range(N_Z)])
        for y in range(1, N_Y)
    ]
    mine = jnp.where(my_y == 0, mine, others[0] + others[1] + others[2])
    around = [mine] + [
        lax.ppermute(mine, "x", [(x, (x + step) % N_X) for x in range(N_X)]) for step in range(1, N_X)
    ]
    around = jnp.stack(around)
    return jnp.stack([pick(around, my_x - x) for x in range(N_X)])


def swap_lead(half, my_core):
    other = lax.ppermute(half, "core", [(0, 1), (1, 0)])
    first = jnp.where(my_core == 0, half, other)
    second = jnp.where(my_core == 0, other, half)
    return jnp.stack([first, second], axis=1).reshape(N_ROW, len(BLOCKS), PIECE, NB)


def col_pairs(moves):
    return [
        (device(2 * a + core, y, z), device(2 * b + core, y, z))
        for a, b, cores in moves
        for core in range(cores)
        for y in range(N_Y)
        for z in range(N_Z)
    ]


def cols_out(strip):
    return send(strip, col_pairs([(0, 1, 2), (1, 2, 1)])), send(strip, col_pairs([(0, 3, 2), (1, 0, 1)]))


def cols_on(up):
    return send(up, col_pairs([(1, 2, 2), (2, 3, 1)]))


def swap_cols(strip, up, down, onward, my_x, my_core):
    own = jnp.where(my_x == 0, strip, jnp.where(my_x == 1, up, jnp.where(my_x == 2, onward, down)))
    last = jnp.where(my_x == 0, down, jnp.where(my_x == 1, strip, jnp.where(my_x == 2, up, onward)))
    other = lax.ppermute(own, "core", [(0, 1), (1, 0)])
    passed = lax.ppermute(last, "core", [(0, 1)])
    first = jnp.where(my_core == 0, own, other)
    second = jnp.where(my_core == 0, other, own)
    last = jnp.where(my_core == 0, last, passed)
    return jnp.concatenate([first, second, last], axis=0)


def body(kernel):
    my_x, my_core = lax.axis_index("x"), lax.axis_index("core")
    my_y, my_z = lax.axis_index("y"), lax.axis_index("z")
    my_row = my_x * N_CORE + my_core
    my_col = my_y * N_Z + my_z
    place = jnp.stack([my_row, my_col, jnp.int32(N_ROW), jnp.int32(N_COL)]).astype(jnp.int32)
    strip = kernel[0:NB]
    parts = scatter_lead(strip, my_x, my_core, my_z)
    strip, parts = lax.optimization_barrier((strip, parts))
    mine = scatter_rows(strip, my_row, my_y, my_z)
    eighth = spread_lead(parts, my_z)
    strip, mine = lax.optimization_barrier((strip, mine))
    gathered = lax.all_gather(mine, ("y", "z")).reshape(N_Y, N_Z, PANELS, 2 * NB // N_Z, NB)
    up, down = cols_out(strip)
    eighth, up, down = lax.optimization_barrier((eighth, up, down))
    onward = cols_on(up)
    quarter = share_lead(eighth, my_x, my_y)
    quarter, onward = lax.optimization_barrier((quarter, onward))
    lead = swap_lead(quarter, my_core)
    cols = swap_cols(strip, up, down, onward, my_x, my_core)
    work, inv = factor_lead(lead)
    high, low = solve_lead(place, work, inv, cols)
    return update(place, kernel, gathered, high, low)


def solution(mesh):
    fine = Mesh(mesh.devices.reshape(N_X, N_CORE, N_Y, N_Z), AXES)
    placed = P(("x", "core"), ("y", "z"))
    return jax.shard_map(body, mesh=fine, in_specs=(placed,), out_specs=placed, check_vma=False)
```

```python
import jax
import jax.numpy as jnp
from jax import lax
from jax.experimental import pallas as pl
from jax.experimental.pallas import tpu as pltpu
from jax.sharding import Mesh
from jax.sharding import PartitionSpec as P

NB = 256
PANELS = 3
LEAD = NB * PANELS
HALF = 128
F32 = jnp.float32
BF16 = jnp.bfloat16


def split(value):
    high = value.astype(BF16)
    return high, (value - high.astype(F32)).astype(BF16)


def dot_split(left, right, left_dim, right_dim):
    left_high, left_low = split(left)
    right_high, right_low = split(right)

    def dot(a, b):
        return lax.dot_general(a, b, (((left_dim,), (right_dim,)), ((), ())), preferred_element_type=F32)

    return dot(left_low, right_high) + dot(left_high, right_low) + dot(left_high, right_high)


def row_of(value, step):
    return jnp.take_along_axis(value, jnp.full(value.shape, step, jnp.int32), axis=0)


def inverse_factor(block):
    groups = HALF // 8
    rows = lax.broadcasted_iota(jnp.int32, (8, HALF), 0)
    lanes = lax.broadcasted_iota(jnp.int32, (8, HALF), 1)
    left = [block[8 * g : 8 * g + 8] for g in range(groups)]
    right = [(lanes == rows + 8 * g).astype(F32) for g in range(groups)]
    for first in range(groups):
        columns = [
            [
                jnp.broadcast_to(left[g][:, 8 * first + j : 8 * first + j + 1], (8, HALF))
                if g >= first
                else None
                for g in range(groups)
            ]
            for j in range(8)
        ]
        pivots = rows.astype(F32)
        for j in range(8):
            pivot = row_of(columns[j][first], j)
            inverse = pl.reciprocal(pivot, approx=True)
            inverse = inverse * (2.0 - pivot * inverse)
            pivots = jnp.where(rows == j, pivot, pivots)
            left_row = row_of(left[first], j)
            right_row = row_of(right[first], j)
            heads = [row_of(columns[i][first], j) for i in range(j + 1, 8)]
            for g in range(first, groups):
                scale = columns[j][g] * inverse
                if g == first:
                    if j == 7:
                        continue
                    scale = jnp.where(rows > j, scale, 0.0)
                for i in range(j + 1, 8):
                    columns[i][g] = columns[i][g] - scale * heads[i - j - 1]
                left[g] = left[g] - scale * left_row
                right[g] = right[g] - scale * right_row
        right[first] = right[first] * lax.rsqrt(pivots)
    return jnp.concatenate(right, 0)


BLOCKS = [(j, j) for j in range(PANELS)] + [((j + 1) % PANELS, j) for j in range(PANELS)]


def factor_kernel(lead_ref, work, inv):
    for slot, (k, j) in enumerate(BLOCKS):
        if k >= j:
            for r in range(8):
                at = k * NB + r * PIECE
                work[at : at + PIECE, j * NB : (j + 1) * NB] = lead_ref[r, slot]
        else:
            turned = lead_ref[:, slot].reshape(NB, NB).T
            work[j * NB : (j + 1) * NB, k * NB : (k + 1) * NB] = turned

    @pl.loop(0, 2 * PANELS)
    def _(p):
        at = pl.multiple_of(p * HALF, HALF)
        inverse = inverse_factor(work[pl.ds(at, HALF), pl.ds(at, HALF)])

        @pl.when(p % 2 == 0)
        def _():
            inv[pl.ds(at, HALF), 0:HALF] = inverse
            inv[pl.ds(at, HALF), HALF:NB] = jnp.zeros_like(inverse)

        @pl.when(p % 2 == 1)
        def _():
            before = pl.multiple_of((p - 1) * HALF, HALF)
            cross = dot_split(work[pl.ds(at, HALF), pl.ds(before, HALF)], inv[pl.ds(before, HALF), 0:HALF], 1, 0)
            inv[pl.ds(at, HALF), 0:HALF] = -dot_split(inverse, cross, 1, 0)
            inv[pl.ds(at, HALF), HALF:NB] = inverse

        for done in range(2 * PANELS - 1):

            @pl.when(p == done)
            def _():
                here = slice(done * HALF, (done + 1) * HALF)
                below = slice((done + 1) * HALF, LEAD)
                factor = dot_split(work[below, here], inverse, 1, 1)
                work[below, here] = factor
                for first in range(below.start, LEAD, NB):
                    rows = slice(first, LEAD)
                    lanes = slice(first, min(first + NB, LEAD))
                    left = factor[first - below.start :]
                    right = factor[first - below.start : lanes.stop - below.start]
                    work[rows, lanes] = work[rows, lanes] - dot_split(left, right, 1, 1)


def factor_lead(lead):
    vmem = pl.BlockSpec(memory_space=pltpu.VMEM)
    return pl.pallas_call(
        factor_kernel,
        out_shape=[jax.ShapeDtypeStruct((LEAD, LEAD), F32), jax.ShapeDtypeStruct((LEAD, NB), F32)],
        in_specs=[vmem],
        out_specs=[vmem, vmem],
        compiler_params=pltpu.CompilerParams(vmem_limit_bytes=24 * 2**20),
        cost_estimate=pl.CostEstimate(flops=20 * 10**9, bytes_accessed=6 * 2**20, transcendentals=0),
        name="factor_lead",
    )(lead)


def solve_kernel(place_ref, work, inv, cols_ref, high_ref, low_ref, rhs):
    my_col = place_ref[1]
    rhs[...] = cols_ref[...]
    for p in range(PANELS):
        here = slice(p * NB, (p + 1) * NB)
        rhs[here] = dot_split(inv[here], rhs[here], 1, 0)
        if p + 1 < PANELS:
            below = slice((p + 1) * NB, LEAD)
            rhs[below] = rhs[below] - dot_split(work[below, here], rhs[here], 1, 0)

    @pl.when(my_col < PANELS)
    def _():
        rows = lax.broadcasted_iota(jnp.int32, (LEAD, NB), 0)
        lanes = lax.broadcasted_iota(jnp.int32, (LEAD, NB), 1)
        rhs[:, 0:NB] = (rows == lanes + my_col * NB).astype(F32)

    for p in reversed(range(PANELS)):
        here = slice(p * NB, (p + 1) * NB)
        solved = dot_split(inv[here].T, rhs[here], 1, 0)
        rhs[here] = solved
        if p > 0:
            above = slice(0, p * NB)
            rhs[above] = rhs[above] - dot_split(work[here, above].T, solved, 1, 0)
    high, low = split(rhs[...])
    high_ref[...] = high
    low_ref[...] = low


def solve_lead(place, work, inv, cols):
    width = cols.shape[1]
    vmem = pl.BlockSpec(memory_space=pltpu.VMEM)
    return pl.pallas_call(
        solve_kernel,
        out_shape=[jax.ShapeDtypeStruct((LEAD, width), BF16)] * 2,
        in_specs=[pl.BlockSpec(memory_space=pltpu.SMEM), vmem, vmem, vmem],
        out_specs=[vmem, vmem],
        scratch_shapes=[pltpu.VMEM((LEAD, width), F32)],
        compiler_params=pltpu.CompilerParams(vmem_limit_bytes=24 * 2**20),
        cost_estimate=pl.CostEstimate(flops=8 * 10**9, bytes_accessed=6 * 2**20, transcendentals=0),
        name="solve_lead",
    )(place, work, inv, cols)


def update_kernel(place_ref, base_ref, rows_ref, high_ref, low_ref, out_ref):
    first_id = place_ref[0] + place_ref[2] * pl.program_id(0)
    near = place_ref[1]
    left = slice(0, NB)
    right = slice(NB, 2 * NB)
    panel = near < PANELS

    def product(rows, span):
        parts = [split(rows_ref[0, rows, k].reshape(-1, NB)) for k in range(PANELS)]
        high = jnp.concatenate([part[0] for part in parts], axis=1)
        low = jnp.concatenate([part[1] for part in parts], axis=1)
        outs = []
        for at in range(0, high.shape[0], HALF):
            some = slice(at, at + HALF)
            total = jnp.dot(low[some], high_ref[:, span], preferred_element_type=F32)
            total = total + jnp.dot(high[some], low_ref[:, span], preferred_element_type=F32)
            outs.append(total + jnp.dot(high[some], high_ref[:, span], preferred_element_type=F32))
        return jnp.concatenate(outs, axis=0)

    @pl.when(first_id >= near)
    def _():
        total = product(slice(0, 8), left).reshape(2, NB, NB)

        @pl.when(panel)
        def _():
            rows = lax.broadcasted_iota(jnp.int32, (NB, NB), 0)
            lanes = lax.broadcasted_iota(jnp.int32, (NB, NB), 1)
            out_ref[0, :, left] = jnp.where((rows >= lanes) | (first_id > near), total[0], 0.0)
            out_ref[1, :, left] = total[1]

        @pl.when(jnp.logical_not(panel))
        def _():
            out_ref[:, :, left] = base_ref[:, :, left] - total

        out_ref[0, :, right] = jnp.zeros((NB, NB), F32)
        out_ref[1, :, right] = base_ref[1, :, right] - product(slice(4, 8), right)

    @pl.when(first_id < near)
    def _():
        out_ref[0] = jnp.zeros((NB, 2 * NB), F32)
        total = product(slice(4, 8), left)
        out_ref[1, :, left] = jnp.where(panel, total, base_ref[1, :, left] - total)
        out_ref[1, :, right] = jnp.zeros((NB, NB), F32)


def update(place, base, gathered, high, low):
    rows, width = base.shape
    pairs = base.reshape(2, rows // 2, width)
    return pl.pallas_call(
        update_kernel,
        grid=(rows // NB // 2,),
        out_shape=jax.ShapeDtypeStruct(pairs.shape, F32),
        in_specs=[
            pl.BlockSpec(memory_space=pltpu.SMEM),
            pl.BlockSpec((2, NB, width), lambda y: (0, y, 0)),
            pl.BlockSpec((1, 8, PANELS, 64, NB), lambda y: (y, 0, 0, 0, 0)),
            pl.BlockSpec(memory_space=pltpu.VMEM),
            pl.BlockSpec(memory_space=pltpu.VMEM),
        ],
        out_specs=pl.BlockSpec((2, NB, width), lambda y: (0, y, 0)),
        compiler_params=pltpu.CompilerParams(vmem_limit_bytes=50 * 2**20),
        cost_estimate=pl.CostEstimate(flops=5 * 10**9, bytes_accessed=16 * 2**20, transcendentals=0),
        name="update",
    )(place, pairs, gathered, high, low).reshape(rows, width)


N_X, N_CORE, N_Y, N_Z = 4, 2, 4, 8
N_ROW = N_X * N_CORE
N_COL = N_Y * N_Z
AXES = ("x", "core", "y", "z")
PIECE = NB // N_Z


def device(row, y, z):
    return (row * N_Y + y) * N_Z + z


def send(value, pairs):
    return lax.ppermute(value, AXES, pairs)


def pick(stacked, index):
    return lax.dynamic_index_in_dim(stacked, index % stacked.shape[0], 0, keepdims=False)


def scatter_rows(strip, my_row, my_y, my_z):
    pieces = strip.T.reshape(N_Z, 2 * NB // N_Z, NB)
    received = []
    for step in range(N_Z):
        pairs = [
            (device(k, y, z), device(z, y, (z + step + k) % N_Z))
            for k in range(PANELS)
            for y in range(N_Y)
            for z in range(N_Z)
        ]
        received.append(send(pick(pieces, my_z + step + my_row), pairs))
    received = jnp.stack(received)
    return jnp.stack([pick(received, my_z - my_row - k) for k in range(PANELS)])


def scatter_lead(strip, my_x, my_core, my_z):
    pieces = strip[:, 0:NB].reshape(N_X, N_CORE, PIECE, NB)
    keep = lax.dynamic_index_in_dim(pieces, my_core, 1, keepdims=False)
    give = lax.dynamic_index_in_dim(pieces, 1 - my_core, 1, keepdims=False)
    got = lax.ppermute(give, "core", [(0, 1), (1, 0)])
    both = jnp.stack(
        [jnp.where(my_core == 0, keep, got), jnp.where(my_core == 0, got, keep)], axis=1
    )
    received = [pick(both, my_x)]
    for step in range(1, N_X):
        pairs = [
            (device(N_CORE * x + core, 0, j), device(N_CORE * ((x + step) % N_X) + core, 0, j))
            for x in range(2)
            for core in range(N_CORE)
            for j in range(PANELS)
        ]
        received.append(send(pick(both, my_x + step), pairs))
    received = jnp.stack(received)
    parts = jnp.concatenate([pick(received, my_x), pick(received, my_x - 1)[0:1]], axis=0)
    return jnp.stack([pick(parts, my_z), pick(parts, my_z + 1)])


def spread_lead(parts, my_z):
    far = send(
        parts, [(device(r, 0, j), device(r, 0, j + N_Z // 2)) for r in range(N_ROW) for j in range(PANELS)]
    )
    hold = jnp.where(my_z >= N_Z // 2, far, parts)
    received = [hold]
    for step in range(1, N_Z // 2):
        pairs = [
            (device(r, 0, j + half), device(r, 0, (j + half + step) % N_Z))
            for r in range(N_ROW)
            for j in range(PANELS)
            for half in (0, N_Z // 2)
        ]
        received.append(send(hold, pairs))
    received = jnp.stack(received)
    spread = [pick(received, my_z - j) for j in range(PANELS)]
    return jnp.stack(spread, axis=1).reshape(len(BLOCKS), PIECE, NB)


def share_lead(mine, my_x, my_y):
    others = [
        send(mine, [(device(r, 0, z), device(r, y, z)) for r in range(N_ROW) for z in range(N_Z)])
        for y in range(1, N_Y)
    ]
    mine = jnp.where(my_y == 0, mine, others[0] + others[1] + others[2])
    around = [mine] + [
        lax.ppermute(mine, "x", [(x, (x + step) % N_X) for x in range(N_X)]) for step in range(1, N_X)
    ]
    around = jnp.stack(around)
    return jnp.stack([pick(around, my_x - x) for x in range(N_X)])


def swap_lead(half, my_core):
    other = lax.ppermute(half, "core", [(0, 1), (1, 0)])
    first = jnp.where(my_core == 0, half, other)
    second = jnp.where(my_core == 0, other, half)
    return jnp.stack([first, second], axis=1).reshape(N_ROW, len(BLOCKS), PIECE, NB)


def col_pairs(moves):
    return [
        (device(2 * a + core, y, z), device(2 * b + core, y, z))
        for a, b, cores in moves
        for core in range(cores)
        for y in range(N_Y)
        for z in range(N_Z)
    ]


def cols_out(strip):
    return send(strip, col_pairs([(0, 1, 2), (1, 2, 1)])), send(strip, col_pairs([(0, 3, 2), (1, 0, 1)]))


def cols_on(up):
    return send(up, col_pairs([(1, 2, 2), (2, 3, 1)]))


def swap_cols(strip, up, down, onward, my_x, my_core):
    own = jnp.where(my_x == 0, strip, jnp.where(my_x == 1, up, jnp.where(my_x == 2, onward, down)))
    last = jnp.where(my_x == 0, down, jnp.where(my_x == 1, strip, jnp.where(my_x == 2, up, onward)))
    other = lax.ppermute(own, "core", [(0, 1), (1, 0)])
    passed = lax.ppermute(last, "core", [(0, 1)])
    first = jnp.where(my_core == 0, own, other)
    second = jnp.where(my_core == 0, other, own)
    last = jnp.where(my_core == 0, last, passed)
    return jnp.concatenate([first, second, last], axis=0)


def body(kernel):
    my_x, my_core = lax.axis_index("x"), lax.axis_index("core")
    my_y, my_z = lax.axis_index("y"), lax.axis_index("z")
    my_row = my_x * N_CORE + my_core
    my_col = my_y * N_Z + my_z
    place = jnp.stack([my_row, my_col, jnp.int32(N_ROW), jnp.int32(N_COL)]).astype(jnp.int32)
    strip = kernel[0:NB]
    parts = scatter_lead(strip, my_x, my_core, my_z)
    strip, parts = lax.optimization_barrier((strip, parts))
    mine = scatter_rows(strip, my_row, my_y, my_z)
    eighth = spread_lead(parts, my_z)
    strip, mine = lax.optimization_barrier((strip, mine))
    gathered = lax.all_gather(mine, ("y", "z")).reshape(N_Y, N_Z, PANELS, 2 * NB // N_Z, NB)
    up, down = cols_out(strip)
    eighth, up, down = lax.optimization_barrier((eighth, up, down))
    onward = cols_on(up)
    quarter = share_lead(eighth, my_x, my_y)
    quarter, onward = lax.optimization_barrier((quarter, onward))
    lead = swap_lead(quarter, my_core)
    cols = swap_cols(strip, up, down, onward, my_x, my_core)
    work, inv = factor_lead(lead)
    high, low = solve_lead(place, work, inv, cols)
    return update(place, kernel, gathered, high, low)


def solution(mesh):
    fine = Mesh(mesh.devices.reshape(N_X, N_CORE, N_Y, N_Z), AXES)
    placed = P(("x", "core"), ("y", "z"))
    return jax.shard_map(body, mesh=fine, in_specs=(placed,), out_specs=placed, check_vma=False)
```
